512 devices in a mesh: queue: 32 (over x, z_hi, core), seq: 16 (over y, z_lo).
Axes of the slice: x: 4, y: 8, z: 8 (z_hi: 4, z_lo: 2; z = z_hi * 2 + z_lo), core: 2. Of those that a mesh axis runs over, the one named last changes fastest.
Arguments:
- query_rows: bfloat16 [32, 2048, 4096], P('queue', 'seq'), may hold values from -140 to 140
- key_rows: bfloat16 [32, 2048, 4096], P('queue', 'seq'), may hold values from -6 to 6
- value_rows: bfloat16 [32, 2048, 4096], P('queue', 'seq'), may hold values from -6 to 6
- level_gains: float32 [50, 4096], replicated, may hold values from 0.1 to 1.9
- noise_levels: int32 [32], P('queue'), may hold values from 0 to 49
- halo_frames: int32 [32], P('queue'), may hold values from 1 to 4, as said below
Outputs:
- advanced: bfloat16 [32, 2048, 4096], P('queue', 'seq')
The draws below stay inside these ranges and needn't reach their ends.
Inputs may be any that keep to these rules, and one draw needn't show every extreme that they name: `halo_frames`: both 1 and 4 are taken by some group other than group 0.
All inputs are finite; a program needn't handle non-finite values.
Results may differ from the reference program's by a relative error of at most 0.0049.
Values may be sent and summed in bfloat16 or wider, within the bound.
A program may use at most 64 MiB of HBM per device.

```python
import jax
import jax.numpy as jnp
from jax import lax

HD = 128
FTOK = 128
HALO = 4
LEVELS = 50
GROUPS = 32
GTOK = 2048
HEADS = 32
HH = 4096


def shared_parts(key):
    base = jnp.clip(jax.random.normal(jax.random.fold_in(key, 11), (GROUPS, GTOK, HH), jnp.float32), -5.5, 5.5)
    return base


def draw_key_rows(key, part):
    base = shared_parts(key)
    return base.astype(jnp.bfloat16)


def draw_query_rows(key, part):
    key = jax.random.fold_in(key, 4)
    return jnp.clip(jax.random.normal(key, (GROUPS, GTOK, HH), jnp.float32), -5.5, 5.5).astype(jnp.bfloat16)


def draw_halo_frames(key, part):
    key = jax.random.fold_in(key, 5)
    counts = jax.random.randint(jax.random.fold_in(key, 1), (GROUPS,), 1, HALO + 1)
    chosen = jax.random.randint(jax.random.fold_in(key, 2), (), 1, GROUPS)
    second = 1 + chosen % (GROUPS - 1)
    counts = counts.at[chosen].set(HALO)
    return counts.at[second].set(1).astype(jnp.int32)


def set_ends(entries, stream_key, least, top_value):
    dims = entries.shape
    place = [jax.random.randint(jax.random.fold_in(stream_key, axis), (), 0, dims[axis]) for axis in range(len(dims))]
    entries = entries.at[tuple(place)].set(least)
    longest = dims.index(max(dims))
    place[longest] = (place[longest] + 1) % dims[longest]
    return entries.at[tuple(place)].set(top_value)


def levels(rng, shape, shards, least, high):
    gain = 1.0
    for position, blocks in shards:
        steps = jax.random.uniform(jax.random.fold_in(jax.random.fold_in(rng, 6), position), (blocks,), jnp.float32, least / len(shards), high / len(shards))
        gain = gain * jnp.repeat(jnp.exp(steps), shape[position] // blocks).reshape((-1,) + (1,) * (len(shape) - 1 - position))
    return gain


def noise(rng, dims, spread, limit, cuts=(), held_as=jnp.bfloat16):
    result = spread * jax.random.normal(rng, dims, jnp.float32)
    if cuts:
        result = result * levels(rng, dims, cuts, -0.22, 0.18)
    return jnp.clip(result, -limit, limit).astype(held_as)


def setup_inputs(seed: int = 0) -> dict:
    streams_of = jax.random.split(jax.random.key(seed), 7)
    query_rows = draw_query_rows(jax.random.fold_in(streams_of[6], 71), 0)
    key_rows = draw_key_rows(jax.random.fold_in(streams_of[6], 71), 0)
    value_rows = noise(streams_of[2], (GROUPS, GTOK, HH), 1.0, 6.0, ((0, 32), (1, 16)))
    level_gains = jnp.clip(1.0 + 0.18 * jax.random.normal(streams_of[3], (LEVELS, HH), jnp.float32), 0.1, 1.9)
    noise_levels = set_ends(jax.random.randint(streams_of[4], (GROUPS,), 0, LEVELS), jax.random.fold_in(streams_of[4], 1), 0, LEVELS - 1).astype(jnp.int32)
    halo_frames = draw_halo_frames(jax.random.fold_in(streams_of[6], 71), 0)
    return {"query_rows": query_rows, "key_rows": key_rows, "value_rows": value_rows, "level_gains": level_gains, "noise_levels": noise_levels, "halo_frames": halo_frames}


def attend_group(queries, key_part, value_part, edge_keys, edge_values, visible, gain_row):
    query_heads = queries.reshape(GTOK, HEADS, HD).transpose(1, 0, 2)
    all_keys = jnp.concatenate([edge_keys, key_part], axis=0).reshape(-1, HEADS, HD).transpose(1, 0, 2)
    all_values = jnp.concatenate([edge_values, value_part], axis=0).reshape(-1, HEADS, HD).transpose(1, 0, 2)
    mask_all = jnp.concatenate([visible > 0, jnp.ones((GTOK,), dtype=bool)], axis=0)
    head_gains = gain_row.reshape(HEADS, HD)
    score_scale = HD ** (-0.5)

    def one_head(packed):
        query_head, key_head, value_head, gain_head = packed
        scores = jnp.dot(query_head, key_head.T, preferred_element_type=jnp.float32) * score_scale
        scores = jnp.where(mask_all[None, :], scores, jnp.float32(-1e+30))
        top_score = lax.optimization_barrier(jnp.max(scores, axis=-1, keepdims=True))
        expon = jnp.exp(scores - top_score)
        weights = (expon / lax.optimization_barrier(jnp.sum(expon, axis=-1, keepdims=True))).astype(jnp.bfloat16)
        mixed = jnp.dot(weights, value_head, preferred_element_type=jnp.float32)
        mean_sq = lax.optimization_barrier(jnp.mean(mixed * mixed, axis=-1, keepdims=True))
        return (mixed * lax.rsqrt(mean_sq + 1e-06) * gain_head[None, :]).astype(jnp.bfloat16)
    normed = lax.map(one_head, (query_heads, all_keys, all_values, head_gains))
    return normed.transpose(1, 0, 2).reshape(GTOK, HH)

def reference(query_rows, key_rows, value_rows, level_gains, noise_levels, halo_frames):
    edge_width = HALO * FTOK
    prev_keys = jnp.roll(key_rows[:, GTOK - edge_width:], 1, axis=0)
    prev_values = jnp.roll(value_rows[:, GTOK - edge_width:], 1, axis=0)
    positions = jnp.arange(edge_width, dtype=jnp.int32)
    group_ids = jnp.arange(GROUPS, dtype=jnp.int32)
    visible = ((positions[None, :] >= (HALO - halo_frames[:, None]) * FTOK) & (group_ids[:, None] > 0)).astype(jnp.int32)
    gain_rows = level_gains[noise_levels]

    def per_group(packed):
        return attend_group(*packed)
    normed = lax.map(per_group, (query_rows, key_rows, value_rows, prev_keys, prev_values, visible, gain_rows))
    return jnp.roll(normed, 1, axis=0)
```

```python
import functools
import math

import jax
import jax.numpy as jnp
from jax import lax
from jax.experimental import pallas as pl
from jax.experimental.pallas import tpu as pltpu
from jax.sharding import PartitionSpec as P

HEADS_DEV = 2
HD = 128
FTOK = 128
HALO = 4
LEVELS = 50
EDGE = HALO * FTOK
MESH = pl.DeviceIdType.MESH
EXP2_SCALE = HD**-0.5 * math.log2(math.e)


def kernel(
    nq,
    ns,
    q_ref,
    k_ref,
    v_ref,
    gains_ref,
    level_ref,
    halo_ref,
    out_ref,
    qbuf,
    kbuf,
    vbuf,
    obuf,
    gbuf,
    q_send,
    k_send,
    v_send,
    q_recv,
    k_recv,
    v_recv,
    halo_send,
    halo_recv,
    out_send,
    out_recv,
    gain_sem,
    ready_sem,
):
    tok = q_ref.shape[0]
    width = HEADS_DEV * HD
    tail = EDGE // tok
    me_q = lax.axis_index("queue")
    me = lax.axis_index("seq")
    nxt = lax.rem(me_q + 1, nq)
    prv = lax.rem(me_q + nq - 1, nq)

    barrier = pltpu.get_barrier_semaphore()

    @pl.loop(1, ns)
    def _(step):
        pl.semaphore_signal(
            barrier, inc=1, device_id=(me_q, lax.rem(me + step, ns)), device_id_type=MESH
        )

    pl.semaphore_signal(barrier, inc=1, device_id=(nxt, me), device_id_type=MESH)
    pl.semaphore_signal(barrier, inc=1, device_id=(prv, me), device_id_type=MESH)

    gain_copy = pltpu.make_async_copy(
        gains_ref.at[:, pl.ds(pl.multiple_of(me * width, width), width)], gbuf, gain_sem
    )
    gain_copy.start()
    pl.semaphore_wait(barrier, ns + 1)

    is_tail = (me >= ns - tail).astype(jnp.int32)

    def kv_dst(buf, h, source):
        return buf.at[h, pl.ds(pl.multiple_of(EDGE + source * tok, tok), tok)]

    def q_dst(h, source):
        return qbuf.at[h, pl.ds(pl.multiple_of(source * tok, tok), tok)]

    def src(ref, h, target):
        return ref.at[:, pl.ds(pl.multiple_of(target * width + h * HD, HD), HD)]

    @pl.loop(0, HEADS_DEV)
    def _(h):
        pltpu.make_async_copy(src(k_ref, h, me), kv_dst(kbuf, h, me), k_recv.at[h, is_tail]).start()
        pltpu.make_async_copy(src(v_ref, h, me), kv_dst(vbuf, h, me), v_recv.at[h, is_tail]).start()
        pltpu.make_async_copy(src(q_ref, h, me), q_dst(h, me), q_recv.at[h, me]).start()

        @pl.loop(1, ns)
        def _(step):
            peer = lax.rem(me + step, ns)
            pltpu.make_async_remote_copy(
                src(k_ref, h, peer), kv_dst(kbuf, h, me), k_send, k_recv.at[h, is_tail],
                device_id=(me_q, peer), device_id_type=MESH,
            ).start()

        @pl.loop(1, ns)
        def _(step):
            peer = lax.rem(me + step, ns)
            pltpu.make_async_remote_copy(
                src(v_ref, h, peer), kv_dst(vbuf, h, me), v_send, v_recv.at[h, is_tail],
                device_id=(me_q, peer), device_id_type=MESH,
            ).start()

        @pl.loop(1, ns)
        def _(step):
            peer = lax.rem(me + step, ns)
            pltpu.make_async_remote_copy(
                src(q_ref, h, peer), q_dst(h, me), q_send, q_recv.at[h, me],
                device_id=(me_q, peer), device_id_type=MESH,
            ).start()

    pl.semaphore_signal(ready_sem, inc=1, device_id=(prv, me), device_id_type=MESH)

    gain_copy.wait()
    gain_row = gbuf[pl.ds(level_ref[0], 1), :]
    first_seen = jnp.where(me_q > 0, HALO - halo_ref[0], HALO)
    frames = lax.broadcasted_iota(jnp.int32, (1, EDGE), 1) // FTOK
    bias = jnp.where(frames >= first_seen, jnp.float32(0), jnp.float32(-1e30))

    def wait_rows(sem, buf, h, first, rows):
        part = buf.at[h, pl.ds(first, rows)]
        pltpu.make_async_copy(part, part, sem).wait()

    def halo_copy(buf, h, i):
        return pltpu.make_async_remote_copy(
            buf.at[h, pl.ds(ns * tok, EDGE)], buf.at[h, pl.ds(0, EDGE)],
            halo_send.at[i, h], halo_recv.at[i, h],
            device_id=(nxt, me), device_id_type=MESH,
        )

    pl.semaphore_wait(ready_sem, 1)

    rows = 2 * tok

    for h in range(HEADS_DEV):
        for i, (buf, recv) in enumerate(((kbuf, k_recv), (vbuf, v_recv))):
            wait_rows(recv.at[h, 1], buf, h, ns * tok, EDGE)
            halo_copy(buf, h, i).start()
        for i, (buf, recv) in enumerate(((kbuf, k_recv), (vbuf, v_recv))):
            wait_rows(recv.at[h, 0], buf, h, EDGE, ns * tok - EDGE)
            halo_copy(buf, h, i).wait_recv()
        gain_head = gain_row[:, h * HD : (h + 1) * HD]

        @pl.loop(0, ns // 2)
        def _(step):
            pair = lax.rem(me // 2 + ns // 2 - step, ns // 2)
            first = pl.multiple_of(pair * rows, rows)
            for j in range(2):
                peer = 2 * pair + j
                pltpu.make_async_copy(q_dst(h, peer), q_dst(h, peer), q_recv.at[h, peer]).wait()
            queries = qbuf[h, pl.ds(first, rows), :]
            scores = lax.dot_general(
                queries, kbuf[h], (((1,), (1,)), ((), ())), preferred_element_type=jnp.float32
            )
            edge = scores[:, :EDGE] + bias
            own = scores[:, EDGE:]
            top = jnp.maximum(
                jnp.max(edge, axis=1, keepdims=True), jnp.max(own, axis=1, keepdims=True)
            )
            edge_w = jnp.exp2((edge - top) * EXP2_SCALE)
            own_w = jnp.exp2((own - top) * EXP2_SCALE)
            total = jnp.sum(edge_w, axis=1, keepdims=True) + jnp.sum(own_w, axis=1, keepdims=True)
            mixed = jnp.dot(
                edge_w.astype(jnp.bfloat16), vbuf[h, :EDGE], preferred_element_type=jnp.float32
            ) + jnp.dot(
                own_w.astype(jnp.bfloat16), vbuf[h, EDGE:], preferred_element_type=jnp.float32
            )
            mixed = mixed / total
            mean_sq = jnp.mean(mixed * mixed, axis=1, keepdims=True)
            normed = mixed * lax.rsqrt(mean_sq + 1e-06) * gain_head
            obuf[h, pl.ds(first, rows), :] = normed.astype(jnp.bfloat16)
            for j in range(2):
                peer = 2 * pair + j
                pltpu.make_async_remote_copy(
                    obuf.at[h, pl.ds(pl.multiple_of(peer * tok, tok), tok)],
                    out_ref.at[:, pl.ds(pl.multiple_of(me * width + h * HD, HD), HD)],
                    out_send, out_recv,
                    device_id=(nxt, peer), device_id_type=MESH,
                ).start()

    for ref, sem in ((q_ref, q_send), (k_ref, k_send), (v_ref, v_send)):
        sent = ref.at[:, pl.ds(0, (ns - 1) * width)]
        pltpu.make_async_copy(sent, sent, sem).wait()
    for h in range(HEADS_DEV):
        for i, buf in enumerate((kbuf, vbuf)):
            halo_copy(buf, h, i).wait_send()
    pltpu.make_async_copy(out_ref, out_ref, out_send).wait()
    pltpu.make_async_copy(out_ref, out_ref, out_recv).wait()


def per_device(query_rows, key_rows, value_rows, level_gains, noise_levels, halo_frames):
    nq, ns = lax.axis_size("queue"), lax.axis_size("seq")
    _, tok, features = query_rows.shape
    group = ns * tok
    flops = 4 * HEADS_DEV * group * (group + EDGE) * HD
    dma = pltpu.SemaphoreType.DMA
    out = pl.pallas_call(
        functools.partial(kernel, nq, ns),
        out_shape=jax.ShapeDtypeStruct((tok, features), jnp.bfloat16),
        in_specs=[pl.BlockSpec(memory_space=pl.ANY)] * 4
        + [pl.BlockSpec(memory_space=pltpu.SMEM)] * 2,
        out_specs=pl.BlockSpec(memory_space=pl.ANY),
        scratch_shapes=[
            pltpu.VMEM((HEADS_DEV, group, HD), jnp.bfloat16),
            pltpu.VMEM((HEADS_DEV, EDGE + group, HD), jnp.bfloat16),
            pltpu.VMEM((HEADS_DEV, EDGE + group, HD), jnp.bfloat16),
            pltpu.VMEM((HEADS_DEV, group, HD), jnp.bfloat16),
            pltpu.VMEM((LEVELS, HEADS_DEV * HD), jnp.float32),
            dma, dma, dma,
            dma((HEADS_DEV, ns)),
            dma((HEADS_DEV, 2)),
            dma((HEADS_DEV, 2)),
            dma((2, HEADS_DEV)),
            dma((2, HEADS_DEV)),
            dma, dma, dma,
            pltpu.SemaphoreType.REGULAR,
        ],
        compiler_params=pltpu.CompilerParams(
            collective_id=0, has_side_effects=True, vmem_limit_bytes=56 * 2**20
        ),
        cost_estimate=pl.CostEstimate(
            flops=flops, bytes_accessed=8 * 2**20, transcendentals=HEADS_DEV * group * (group + EDGE)
        ),
    )(
        query_rows.reshape(tok, features),
        key_rows.reshape(tok, features),
        value_rows.reshape(tok, features),
        level_gains,
        noise_levels,
        halo_frames,
    )
    return out.reshape(1, tok, features)


def solution(mesh):
    placed = (
        P("queue", "seq", None),
        P("queue", "seq", None),
        P("queue", "seq", None),
        P(),
        P("queue"),
        P("queue"),
    )
    return jax.shard_map(
        per_device, mesh=mesh, in_specs=placed, out_specs=P("queue", "seq", None), check_vma=False
    )
```

```python
import functools
import math

import jax
import jax.numpy as jnp
from jax import lax
from jax.experimental import pallas as pl
from jax.experimental.pallas import tpu as pltpu
from jax.sharding import PartitionSpec as P

HEADS_DEV = 2
HD = 128
FTOK = 128
HALO = 4
LEVELS = 50
EDGE = HALO * FTOK
STAR = 0
MESH = pl.DeviceIdType.MESH
EXP2_SCALE = HD**-0.5 * math.log2(math.e)


def kernel(
    nq,
    ns,
    q_ref,
    k_ref,
    v_ref,
    gains_ref,
    level_ref,
    halo_ref,
    out_ref,
    qbuf,
    kbuf,
    vbuf,
    obuf,
    gbuf,
    q_send,
    k_send,
    v_send,
    q_recv,
    k_recv,
    v_recv,
    halo_send,
    halo_recv,
    out_send,
    out_recv,
    gain_sem,
    ready_sem,
    star_sem,
):
    tok = q_ref.shape[0]
    width = HEADS_DEV * HD
    tail = EDGE // tok
    me_q = lax.axis_index("queue")
    me = lax.axis_index("seq")
    nxt = lax.rem(me_q + 1, nq)
    prv = lax.rem(me_q + nq - 1, nq)

    barrier = pltpu.get_barrier_semaphore()
    is_star = me == STAR

    @pl.loop(1, ns)
    def _(step):
        peer = lax.rem(me + step, ns)

        @pl.when(peer != STAR)
        def _():
            pl.semaphore_signal(barrier, inc=1, device_id=(me_q, peer), device_id_type=MESH)

    gain_copy = pltpu.make_async_copy(
        gains_ref.at[:, pl.ds(pl.multiple_of(me * width, width), width)], gbuf, gain_sem
    )
    gain_copy.start()

    @pl.when(is_star)
    def _():
        pl.semaphore_signal(barrier, inc=1, device_id=(nxt, STAR), device_id_type=MESH)
        pl.semaphore_wait(star_sem, ns - 1)

    @pl.when(jnp.logical_not(is_star))
    def _():
        pl.semaphore_wait(barrier, ns - 1)
        pl.semaphore_signal(star_sem, inc=1, device_id=(me_q, STAR), device_id_type=MESH)

    is_tail = (me >= ns - tail).astype(jnp.int32)
    ny = ns // 2
    row, side = me // 2, lax.rem(me, 2)

    def offset(step):
        return jnp.where(lax.rem(step, 2) == 1, (step + 1) // 2, ny - step // 2)

    def kv_dst(buf, h, source):
        return buf.at[h, pl.ds(pl.multiple_of(EDGE + source * tok, tok), tok)]

    def q_dst(buf, h, source):
        return buf.at[h, pl.ds(pl.multiple_of(source * tok, tok), tok)]

    def src(ref, h, target):
        return ref.at[:, pl.ds(pl.multiple_of(target * width + h * HD, HD), HD)]

    def send(ref, buf, dst, sem, done, h, peer):
        pltpu.make_async_remote_copy(
            src(ref, h, peer), dst(buf, h, me), sem, done, device_id=(me_q, peer), device_id_type=MESH
        ).start()

    def send_pair(ref, buf, dst, sem, done, h, step):
        pair = lax.rem(row + offset(step), ny)
        send(ref, buf, dst, sem, done, h, 2 * pair + side)
        send(ref, buf, dst, sem, done, h, 2 * pair + 1 - side)

    def send_first(ref, buf, dst, sem, done, h):
        pltpu.make_async_copy(src(ref, h, me), dst(buf, h, me), done).start()
        send(ref, buf, dst, sem, done, h, 2 * row + 1 - side)

    def parts(h):
        return (
            (k_ref, kbuf, kv_dst, k_send, k_recv.at[h, is_tail], h),
            (v_ref, vbuf, kv_dst, v_send, v_recv.at[h, is_tail], h),
            (q_ref, qbuf, q_dst, q_send, q_recv.at[h, me], h),
        )

    def send_all(part):
        send_first(*part)

        @pl.loop(1, ny)
        def _(step):
            send_pair(*part, step)

    (keys0, values0, queries0), (keys1, values1, queries1) = parts(0), parts(1)
    send_all(keys0)
    send_all(values0)

    @pl.when(is_star)
    def _():
        pl.semaphore_wait(barrier, 1)
        pl.semaphore_signal(ready_sem, inc=1, device_id=(prv, STAR), device_id_type=MESH)
        pl.semaphore_wait(ready_sem, 1)

        @pl.loop(1, ns)
        def _(step):
            pl.semaphore_signal(
                ready_sem, inc=1, device_id=(me_q, lax.rem(me + step, ns)), device_id_type=MESH
            )

    @pl.when(jnp.logical_not(is_star))
    def _():
        pl.semaphore_wait(ready_sem, 1)

    gain_copy.wait()
    gain_row = gbuf[pl.ds(level_ref[0], 1), :]
    first_seen = jnp.where(me_q > 0, HALO - halo_ref[0], HALO)
    frames = lax.broadcasted_iota(jnp.int32, (1, EDGE), 1) // FTOK
    bias = jnp.where(frames >= first_seen, jnp.float32(0), jnp.float32(-1e30))

    def wait_rows(sem, buf, h, first, rows):
        part = buf.at[h, pl.ds(first, rows)]
        pltpu.make_async_copy(part, part, sem).wait()

    def halo_copy(buf, h, i):
        return pltpu.make_async_remote_copy(
            buf.at[h, pl.ds(ns * tok, EDGE)], buf.at[h, pl.ds(0, EDGE)],
            halo_send.at[i, h], halo_recv.at[i, h],
            device_id=(nxt, me), device_id_type=MESH,
        )

    rows = 2 * tok

    def place(step):
        pair = lax.rem(row + 2 * ny - offset(step), ny)
        return pair, pl.multiple_of(pair * rows, rows)

    def forward_halo(h, i):
        buf, recv = ((kbuf, k_recv), (vbuf, v_recv))[i]
        wait_rows(recv.at[h, 1], buf, h, ns * tok, EDGE)
        halo_copy(buf, h, i).start()

    def wait_keys(h):
        for i, (buf, recv) in enumerate(((kbuf, k_recv), (vbuf, v_recv))):
            wait_rows(recv.at[h, 0], buf, h, EDGE, ns * tok - EDGE)
            halo_copy(buf, h, i).wait_recv()

    def attend(h, step):
        pair, first = place(step)
        for j in range(2):
            part = q_dst(qbuf, h, 2 * pair + j)
            pltpu.make_async_copy(part, part, q_recv.at[h, 2 * pair + j]).wait()
        queries = qbuf[h, pl.ds(first, rows), :]
        scores = lax.dot_general(
            queries, kbuf[h], (((1,), (1,)), ((), ())), preferred_element_type=jnp.float32
        )
        edge = scores[:, :EDGE] + bias
        own = scores[:, EDGE:]
        top = jnp.maximum(
            jnp.max(edge, axis=1, keepdims=True), jnp.max(own, axis=1, keepdims=True)
        )
        edge_w = jnp.exp2((edge - top) * EXP2_SCALE)
        own_w = jnp.exp2((own - top) * EXP2_SCALE)
        total = jnp.sum(edge_w, axis=1, keepdims=True) + jnp.sum(own_w, axis=1, keepdims=True)
        mixed = jnp.dot(
            edge_w.astype(jnp.bfloat16), vbuf[h, :EDGE], preferred_element_type=jnp.float32
        ) + jnp.dot(
            own_w.astype(jnp.bfloat16), vbuf[h, EDGE:], preferred_element_type=jnp.float32
        )
        mixed = mixed / total
        mean_sq = jnp.mean(mixed * mixed, axis=1, keepdims=True)
        normed = mixed * lax.rsqrt(mean_sq + 1e-06) * gain_row[:, h * HD : (h + 1) * HD]
        obuf[h, pl.ds(first, rows), :] = normed.astype(jnp.bfloat16)

    def send_out(h, step):
        pair, _ = place(step)
        for j in range(2):
            peer = 2 * pair + j
            pltpu.make_async_remote_copy(
                obuf.at[h, pl.ds(pl.multiple_of(peer * tok, tok), tok)],
                out_ref.at[:, pl.ds(pl.multiple_of(me * width + h * HD, HD), HD)],
                out_send, out_recv,
                device_id=(nxt, peer), device_id_type=MESH,
            ).start()

    forward_halo(0, 0)
    send_all(keys1)
    forward_halo(0, 1)
    send_all(values1)
    forward_halo(1, 0)
    send_all(queries0)
    forward_halo(1, 1)
    send_all(queries1)

    for h in range(HEADS_DEV):
        wait_keys(h)

        @pl.loop(0, ny)
        def _(step):
            attend(h, step)
            send_out(h, step)

    for ref, sem in ((q_ref, q_send), (k_ref, k_send), (v_ref, v_send)):
        sent = ref.at[:, pl.ds(0, (ns - 1) * width)]
        pltpu.make_async_copy(sent, sent, sem).wait()
    for h in range(HEADS_DEV):
        for i, buf in enumerate((kbuf, vbuf)):
            halo_copy(buf, h, i).wait_send()
    pltpu.make_async_copy(out_ref, out_ref, out_send).wait()
    pltpu.make_async_copy(out_ref, out_ref, out_recv).wait()


def per_device(query_rows, key_rows, value_rows, level_gains, noise_levels, halo_frames):
    nq, ns = lax.axis_size("queue"), lax.axis_size("seq")
    _, tok, features = query_rows.shape
    group = ns * tok
    flops = 4 * HEADS_DEV * group * (group + EDGE) * HD
    dma = pltpu.SemaphoreType.DMA
    out = pl.pallas_call(
        functools.partial(kernel, nq, ns),
        out_shape=pltpu.VMEM((tok, features), jnp.bfloat16),
        in_specs=[pl.BlockSpec(memory_space=pl.ANY)] * 4
        + [pl.BlockSpec(memory_space=pltpu.SMEM)] * 2,
        out_specs=pl.BlockSpec(memory_space=pl.ANY),
        scratch_shapes=[
            pltpu.VMEM((HEADS_DEV, group, HD), jnp.bfloat16),
            pltpu.VMEM((HEADS_DEV, EDGE + group, HD), jnp.bfloat16),
            pltpu.VMEM((HEADS_DEV, EDGE + group, HD), jnp.bfloat16),
            pltpu.VMEM((HEADS_DEV, group, HD), jnp.bfloat16),
            pltpu.VMEM((LEVELS, HEADS_DEV * HD), jnp.float32),
            dma, dma, dma,
            dma((HEADS_DEV, ns)),
            dma((HEADS_DEV, 2)),
            dma((HEADS_DEV, 2)),
            dma((2, HEADS_DEV)),
            dma((2, HEADS_DEV)),
            dma, dma, dma,
            pltpu.SemaphoreType.REGULAR,
            pltpu.SemaphoreType.REGULAR,
        ],
        compiler_params=pltpu.CompilerParams(
            collective_id=0, has_side_effects=True, vmem_limit_bytes=56 * 2**20
        ),
        cost_estimate=pl.CostEstimate(
            flops=flops, bytes_accessed=8 * 2**20, transcendentals=HEADS_DEV * group * (group + EDGE)
        ),
    )(
        query_rows.reshape(tok, features),
        key_rows.reshape(tok, features),
        value_rows.reshape(tok, features),
        level_gains,
        noise_levels,
        halo_frames,
    )
    return out.reshape(1, tok, features)


def solution(mesh):
    placed = (
        P("queue", "seq", None),
        P("queue", "seq", None),
        P("queue", "seq", None),
        P(),
        P("queue"),
        P("queue"),
    )
    return jax.shard_map(
        per_device, mesh=mesh, in_specs=placed, out_specs=P("queue", "seq", None), check_vma=False
    )
```

```python
import functools
import math

import jax
import jax.numpy as jnp
from jax import lax
from jax.experimental import pallas as pl
from jax.experimental.pallas import tpu as pltpu
from jax.sharding import PartitionSpec as P

HEADS_DEV = 2
HD = 128
FTOK = 128
HALO = 4
LEVELS = 50
EDGE = HALO * FTOK
STAR = 0
RUN = 4
TURNS = (0, 2, 6, 4, 3, 5, 1, 7)
KEY_BLOCK = 1024
MESH = pl.DeviceIdType.MESH
EXP2_SCALE = HD**-0.5 * math.log2(math.e)


def kernel(
    nq,
    ns,
    q_ref,
    k_ref,
    v_ref,
    gains_ref,
    level_ref,
    halo_ref,
    out_ref,
    qbuf,
    kbuf,
    vbuf,
    obuf,
    gbuf,
    q_send,
    k_send,
    v_send,
    q_recv,
    k_recv,
    v_recv,
    halo_send,
    halo_recv,
    out_send,
    out_recv,
    gain_sem,
    ready_sem,
    star_sem,
    go_sem,
):
    tok = q_ref.shape[0]
    width = HEADS_DEV * HD
    tail = EDGE // tok
    me_q = lax.axis_index("queue")
    me = lax.axis_index("seq")
    nxt = lax.rem(me_q + 1, nq)
    prv = lax.rem(me_q + nq - 1, nq)

    barrier = pltpu.get_barrier_semaphore()
    is_star = me == STAR

    @pl.loop(1, ns)
    def _(step):
        peer = lax.rem(me + step, ns)

        @pl.when(peer != STAR)
        def _():
            pl.semaphore_signal(barrier, inc=1, device_id=(me_q, peer), device_id_type=MESH)

    gain_copy = pltpu.make_async_copy(
        gains_ref.at[:, pl.ds(pl.multiple_of(me * width, width), width)], gbuf, gain_sem
    )
    gain_copy.start()

    @pl.when(is_star)
    def _():
        pl.semaphore_signal(barrier, inc=1, device_id=(nxt, STAR), device_id_type=MESH)
        pl.semaphore_wait(star_sem, ns - 1)

    @pl.when(jnp.logical_not(is_star))
    def _():
        pl.semaphore_wait(barrier, ns - 1)
        pl.semaphore_signal(star_sem, inc=1, device_id=(me_q, STAR), device_id_type=MESH)

    is_tail = (me >= ns - tail).astype(jnp.int32)
    ny = ns // 2
    row, side = me // 2, lax.rem(me, 2)

    def offset(step):
        return sum(jnp.where(step == i, turn, 0) for i, turn in enumerate(TURNS))

    def kv_dst(buf, h, source):
        return buf.at[h, pl.ds(pl.multiple_of(EDGE + source * tok, tok), tok)]

    def q_dst(buf, h, source):
        return buf.at[h, pl.ds(pl.multiple_of(source * tok, tok), tok)]

    def src(ref, h, target):
        return ref.at[:, pl.ds(pl.multiple_of(target * width + h * HD, HD), HD)]

    def send(ref, buf, dst, sem, done, h, peer):
        pltpu.make_async_remote_copy(
            src(ref, h, peer), dst(buf, h, me), sem, done, device_id=(me_q, peer), device_id_type=MESH
        ).start()

    def send_pair(ref, buf, dst, sem, done, h, step):
        pair = lax.rem(row + offset(step), ny)
        send(ref, buf, dst, sem, done, h, 2 * pair + side)
        send(ref, buf, dst, sem, done, h, 2 * pair + 1 - side)

    def send_first(ref, buf, dst, sem, done, h):
        pltpu.make_async_copy(src(ref, h, me), dst(buf, h, me), done).start()
        send(ref, buf, dst, sem, done, h, 2 * row + 1 - side)

    def parts(h):
        return (
            (k_ref, kbuf, kv_dst, k_send, k_recv.at[h, is_tail], h),
            (v_ref, vbuf, kv_dst, v_send, v_recv.at[h, is_tail], h),
            (q_ref, qbuf, q_dst, q_send, q_recv.at[h, me], h),
        )

    def send_all(part):
        send_first(*part)

        @pl.loop(1, ny)
        def _(step):
            send_pair(*part, step)

    (keys0, values0, queries0), (keys1, values1, queries1) = parts(0), parts(1)
    send_all(keys0)
    send_all(values0)

    @pl.when(is_star)
    def _():
        pl.semaphore_wait(barrier, 1)
        pl.semaphore_signal(ready_sem, inc=1, device_id=(prv, STAR), device_id_type=MESH)
        pl.semaphore_wait(ready_sem, 1)

        @pl.loop(1, ns)
        def _(step):
            pl.semaphore_signal(
                ready_sem, inc=1, device_id=(me_q, lax.rem(me + step, ns)), device_id_type=MESH
            )

    @pl.when(jnp.logical_not(is_star))
    def _():
        pl.semaphore_wait(ready_sem, 1)

    gain_copy.wait()
    gain_row = gbuf[pl.ds(level_ref[0], 1), :]
    first_seen = jnp.where(me_q > 0, HALO - halo_ref[0], HALO)
    frames = lax.broadcasted_iota(jnp.int32, (1, EDGE), 1) // FTOK
    bias = jnp.where(frames >= first_seen, jnp.float32(0), jnp.float32(-1e30))

    def wait_rows(sem, buf, h, first, rows):
        part = buf.at[h, pl.ds(first, rows)]
        pltpu.make_async_copy(part, part, sem).wait()

    def halo_copy(buf, h, i):
        return pltpu.make_async_remote_copy(
            buf.at[h, pl.ds(ns * tok, EDGE)], buf.at[h, pl.ds(0, EDGE)],
            halo_send.at[i, h], halo_recv.at[i, h],
            device_id=(nxt, me), device_id_type=MESH,
        )

    rows = 2 * tok
    keys_all = EDGE + ns * tok

    def place(step):
        pair = lax.rem(row + 2 * ny - offset(step), ny)
        return pair, pl.multiple_of(pair * rows, rows)

    def forward_halo(h, i):
        buf, recv = ((kbuf, k_recv), (vbuf, v_recv))[i]
        wait_rows(recv.at[h, 1], buf, h, ns * tok, EDGE)
        halo_copy(buf, h, i).start()

    def wait_keys(h):
        for i, (buf, recv) in enumerate(((kbuf, k_recv), (vbuf, v_recv))):
            wait_rows(recv.at[h, 0], buf, h, EDGE, ns * tok - EDGE)
            halo_copy(buf, h, i).wait_recv()

    def attend(h, step):
        firsts = []
        for i in range(2):
            pair, first = place(2 * step + i)
            firsts.append(first)
            for j in range(2):
                part = q_dst(qbuf, h, 2 * pair + j)
                pltpu.make_async_copy(part, part, q_recv.at[h, 2 * pair + j]).wait()
        queries = jnp.concatenate([qbuf[h, pl.ds(first, rows), :] for first in firsts], axis=0)
        acc = top = None
        for start in range(0, keys_all, KEY_BLOCK):
            size = min(KEY_BLOCK, keys_all - start)
            scores = lax.dot_general(
                queries, kbuf[h, start : start + size], (((1,), (1,)), ((), ())),
                preferred_element_type=jnp.float32,
            )
            if start == 0:
                scores = jnp.concatenate([scores[:, :EDGE] + bias, scores[:, EDGE:]], axis=1)
            peak = jnp.max(scores, axis=1, keepdims=True)
            new_top = peak if top is None else jnp.maximum(top, peak)
            weights = jnp.exp2((scores - new_top) * EXP2_SCALE).astype(jnp.bfloat16)
            values = jnp.concatenate(
                [vbuf[h, start : start + size], jnp.ones((size, HD), jnp.bfloat16)], axis=1
            )
            part = jnp.dot(weights, values, preferred_element_type=jnp.float32)
            acc = part if acc is None else acc * jnp.exp2((top - new_top) * EXP2_SCALE) + part
            top = new_top
        mixed = acc[:, :HD] / acc[:, HD:]
        mean_sq = jnp.mean(mixed * mixed, axis=1, keepdims=True)
        normed = mixed * lax.rsqrt(mean_sq + 1e-06) * gain_row[:, h * HD : (h + 1) * HD]
        for i, first in enumerate(firsts):
            obuf[h, pl.ds(first, rows), :] = normed[i * rows : (i + 1) * rows].astype(jnp.bfloat16)

    def send_out(h, step):
        pair, _ = place(step)
        for j in range(2):
            peer = 2 * pair + j
            pltpu.make_async_remote_copy(
                obuf.at[h, pl.ds(pl.multiple_of(peer * tok, tok), tok)],
                out_ref.at[:, pl.ds(pl.multiple_of(me * width + h * HD, HD), HD)],
                out_send, out_recv,
                device_id=(nxt, peer), device_id_type=MESH,
            ).start()

    ahead = lax.rem(me_q, 2) == 1
    behind = jnp.logical_not(ahead)
    last_chip = lax.rem(me_q // 2, RUN) == RUN - 1

    forward_halo(0, 0)
    send_all(keys1)
    forward_halo(0, 1)
    send_all(values1)
    forward_halo(1, 0)

    @pl.when(ahead)
    def _():
        send_all(queries0)

    forward_halo(1, 1)

    @pl.when(behind)
    def _():
        pl.semaphore_wait(go_sem, 1)
        send_all(queries0)

    for h in range(HEADS_DEV):
        wait_keys(h)

        if h == 0:

            @pl.when(jnp.logical_and(ahead, jnp.logical_not(last_chip)))
            def _():
                pl.semaphore_signal(go_sem, inc=1, device_id=(prv, me), device_id_type=MESH)

        @pl.loop(0, ny // 2)
        def _(step):
            attend(h, step)
            send_out(h, 2 * step)
            send_out(h, 2 * step + 1)

            if h + 1 < HEADS_DEV:
                @pl.when(step == 0)
                def _():
                    send_first(*queries1)

                @pl.when(step > 0)
                def _():
                    send_pair(*queries1, 2 * step)

                send_pair(*queries1, 2 * step + 1)

            if h == 0:

                @pl.when(jnp.logical_and(jnp.logical_and(ahead, last_chip), step == 2))
                def _():
                    pl.semaphore_signal(go_sem, inc=1, device_id=(prv, me), device_id_type=MESH)

    for ref, sem in ((q_ref, q_send), (k_ref, k_send), (v_ref, v_send)):
        sent = ref.at[:, pl.ds(0, (ns - 1) * width)]
        pltpu.make_async_copy(sent, sent, sem).wait()
    for h in range(HEADS_DEV):
        for i, buf in enumerate((kbuf, vbuf)):
            halo_copy(buf, h, i).wait_send()
    pltpu.make_async_copy(out_ref, out_ref, out_send).wait()
    pltpu.make_async_copy(out_ref, out_ref, out_recv).wait()


def per_device(query_rows, key_rows, value_rows, level_gains, noise_levels, halo_frames):
    nq, ns = lax.axis_size("queue"), lax.axis_size("seq")
    _, tok, features = query_rows.shape
    group = ns * tok
    flops = 4 * HEADS_DEV * group * (group + EDGE) * HD
    dma = pltpu.SemaphoreType.DMA
    out = pl.pallas_call(
        functools.partial(kernel, nq, ns),
        out_shape=pltpu.VMEM((tok, features), jnp.bfloat16),
        in_specs=[pl.BlockSpec(memory_space=pl.ANY)] * 4
        + [pl.BlockSpec(memory_space=pltpu.SMEM)] * 2,
        out_specs=pl.BlockSpec(memory_space=pl.ANY),
        scratch_shapes=[
            pltpu.VMEM((HEADS_DEV, group, HD), jnp.bfloat16),
            pltpu.VMEM((HEADS_DEV, EDGE + group, HD), jnp.bfloat16),
            pltpu.VMEM((HEADS_DEV, EDGE + group, HD), jnp.bfloat16),
            pltpu.VMEM((HEADS_DEV, group, HD), jnp.bfloat16),
            pltpu.VMEM((LEVELS, HEADS_DEV * HD), jnp.float32),
            dma, dma, dma,
            dma((HEADS_DEV, ns)),
            dma((HEADS_DEV, 2)),
            dma((HEADS_DEV, 2)),
            dma((2, HEADS_DEV)),
            dma((2, HEADS_DEV)),
            dma, dma, dma,
            pltpu.SemaphoreType.REGULAR,
            pltpu.SemaphoreType.REGULAR,
            pltpu.SemaphoreType.REGULAR,
        ],
        compiler_params=pltpu.CompilerParams(
            collective_id=0, has_side_effects=True, vmem_limit_bytes=56 * 2**20
        ),
        cost_estimate=pl.CostEstimate(
            flops=flops, bytes_accessed=8 * 2**20, transcendentals=HEADS_DEV * group * (group + EDGE)
        ),
    )(
        query_rows.reshape(tok, features),
        key_rows.reshape(tok, features),
        value_rows.reshape(tok, features),
        level_gains,
        noise_levels,
        halo_frames,
    )
    return out.reshape(1, tok, features)


def solution(mesh):
    placed = (
        P("queue", "seq", None),
        P("queue", "seq", None),
        P("queue", "seq", None),
        P(),
        P("queue"),
        P("queue"),
    )
    return jax.shard_map(
        per_device, mesh=mesh, in_specs=placed, out_specs=P("queue", "seq", None), check_vma=False
    )
```

```python
import functools
import math

import jax
import jax.numpy as jnp
from jax import lax
from jax.experimental import pallas as pl
from jax.experimental.pallas import tpu as pltpu
from jax.sharding import PartitionSpec as P

HEADS_DEV = 2
HD = 128
FTOK = 128
HALO = 4
LEVELS = 50
EDGE = HALO * FTOK
STAR = 0
RUN = 4
TURNS = (0, 2, 6, 4, 3, 5, 1, 7)
KEY_BLOCK = 1024
MESH = pl.DeviceIdType.MESH
EXP2_SCALE = HD**-0.5 * math.log2(math.e)


def kernel(
    nq,
    ns,
    q_ref,
    k_ref,
    v_ref,
    gains_ref,
    level_ref,
    halo_ref,
    out_ref,
    qbuf,
    kbuf,
    vbuf,
    obuf,
    gbuf,
    q_send,
    k_send,
    v_send,
    q_recv,
    k_recv,
    v_recv,
    halo_send,
    halo_recv,
    out_send,
    out_recv,
    gain_sem,
    ready_sem,
    star_sem,
    go_sem,
):
    tok = q_ref.shape[0]
    width = HEADS_DEV * HD
    tail = EDGE // tok
    me_q = lax.axis_index("queue")
    me = lax.axis_index("seq")
    nxt = lax.rem(me_q + 1, nq)
    prv = lax.rem(me_q + nq - 1, nq)

    barrier = pltpu.get_barrier_semaphore()
    is_star = me == STAR

    @pl.loop(1, ns)
    def _(step):
        peer = lax.rem(me + step, ns)

        @pl.when(peer != STAR)
        def _():
            pl.semaphore_signal(barrier, inc=1, device_id=(me_q, peer), device_id_type=MESH)

    gain_copy = pltpu.make_async_copy(
        gains_ref.at[:, pl.ds(pl.multiple_of(me * width, width), width)], gbuf, gain_sem
    )
    gain_copy.start()

    @pl.when(is_star)
    def _():
        pl.semaphore_signal(barrier, inc=1, device_id=(nxt, STAR), device_id_type=MESH)
        pl.semaphore_wait(star_sem, ns - 1)

    @pl.when(jnp.logical_not(is_star))
    def _():
        pl.semaphore_wait(barrier, ns - 1)
        pl.semaphore_signal(star_sem, inc=1, device_id=(me_q, STAR), device_id_type=MESH)

    is_tail = (me >= ns - tail).astype(jnp.int32)
    ny = ns // 2
    row, side = me // 2, lax.rem(me, 2)

    def offset(step):
        return sum(jnp.where(step == i, turn, 0) for i, turn in enumerate(TURNS))

    def kv_dst(buf, h, source):
        return buf.at[h, pl.ds(pl.multiple_of(EDGE + source * tok, tok), tok)]

    def q_dst(buf, h, source):
        return buf.at[h, pl.ds(pl.multiple_of(source * tok, tok), tok)]

    def src(ref, h, target):
        return ref.at[:, pl.ds(pl.multiple_of(target * width + h * HD, HD), HD)]

    def send(ref, buf, dst, sem, done, h, peer):
        pltpu.make_async_remote_copy(
            src(ref, h, peer), dst(buf, h, me), sem, done, device_id=(me_q, peer), device_id_type=MESH
        ).start()

    def send_pair(ref, buf, dst, sem, done, h, step):
        pair = lax.rem(row + offset(step), ny)
        send(ref, buf, dst, sem, done, h, 2 * pair + side)
        send(ref, buf, dst, sem, done, h, 2 * pair + 1 - side)

    def send_first(ref, buf, dst, sem, done, h):
        pltpu.make_async_copy(src(ref, h, me), dst(buf, h, me), done).start()
        send(ref, buf, dst, sem, done, h, 2 * row + 1 - side)

    def parts(h):
        return (
            (k_ref, kbuf, kv_dst, k_send, k_recv.at[h, is_tail], h),
            (v_ref, vbuf, kv_dst, v_send, v_recv.at[h, is_tail], h),
            (q_ref, qbuf, q_dst, q_send, q_recv.at[h, me], h),
        )

    def send_all(part):
        send_first(*part)

        @pl.loop(1, ny)
        def _(step):
            send_pair(*part, step)

    (keys0, values0, queries0), (keys1, values1, queries1) = parts(0), parts(1)
    send_all(keys0)
    send_all(values0)

    @pl.when(is_star)
    def _():
        pl.semaphore_wait(barrier, 1)
        pl.semaphore_signal(ready_sem, inc=1, device_id=(prv, STAR), device_id_type=MESH)
        pl.semaphore_wait(ready_sem, 1)

        @pl.loop(1, ns)
        def _(step):
            pl.semaphore_signal(
                ready_sem, inc=1, device_id=(me_q, lax.rem(me + step, ns)), device_id_type=MESH
            )

    @pl.when(jnp.logical_not(is_star))
    def _():
        pl.semaphore_wait(ready_sem, 1)

    gain_copy.wait()
    gain_row = gbuf[pl.ds(level_ref[0], 1), :]
    first_seen = jnp.where(me_q > 0, HALO - halo_ref[0], HALO)
    frames = lax.broadcasted_iota(jnp.int32, (1, EDGE), 1) // FTOK
    bias = jnp.where(frames >= first_seen, jnp.float32(0), jnp.float32(-1e30))

    def wait_rows(sem, buf, h, first, rows):
        part = buf.at[h, pl.ds(first, rows)]
        pltpu.make_async_copy(part, part, sem).wait()

    def halo_copy(buf, h, i):
        return pltpu.make_async_remote_copy(
            buf.at[h, pl.ds(ns * tok, EDGE)], buf.at[h, pl.ds(0, EDGE)],
            halo_send.at[i, h], halo_recv.at[i, h],
            device_id=(nxt, me), device_id_type=MESH,
        )

    rows = 2 * tok
    keys_all = EDGE + ns * tok

    def place(step):
        pair = lax.rem(row + 2 * ny - offset(step), ny)
        return pair, pl.multiple_of(pair * rows, rows)

    def forward_halo(h, i):
        buf, recv = ((kbuf, k_recv), (vbuf, v_recv))[i]
        wait_rows(recv.at[h, 1], buf, h, ns * tok, EDGE)
        halo_copy(buf, h, i).start()

    def wait_keys(h):
        for i, (buf, recv) in enumerate(((kbuf, k_recv), (vbuf, v_recv))):
            wait_rows(recv.at[h, 0], buf, h, EDGE, ns * tok - EDGE)
            halo_copy(buf, h, i).wait_recv()

    def attend(h, step):
        firsts = []
        for i in range(2):
            pair, first = place(2 * step + i)
            firsts.append(first)
            for j in range(2):
                part = q_dst(qbuf, h, 2 * pair + j)
                pltpu.make_async_copy(part, part, q_recv.at[h, 2 * pair + j]).wait()
        queries = jnp.concatenate([qbuf[h, pl.ds(first, rows), :] for first in firsts], axis=0)
        acc = top = None
        for start in range(0, keys_all, KEY_BLOCK):
            size = min(KEY_BLOCK, keys_all - start)
            scores = lax.dot_general(
                queries, kbuf[h, start : start + size], (((1,), (1,)), ((), ())),
                preferred_element_type=jnp.float32,
            )
            if start == 0:
                scores = jnp.concatenate([scores[:, :EDGE] + bias, scores[:, EDGE:]], axis=1)
            peak = jnp.max(scores, axis=1, keepdims=True)
            new_top = peak if top is None else jnp.maximum(top, peak)
            weights = jnp.exp2((scores - new_top) * EXP2_SCALE).astype(jnp.bfloat16)
            values = jnp.concatenate(
                [vbuf[h, start : start + size], jnp.ones((size, HD), jnp.bfloat16)], axis=1
            )
            part = jnp.dot(weights, values, preferred_element_type=jnp.float32)
            acc = part if acc is None else acc * jnp.exp2((top - new_top) * EXP2_SCALE) + part
            top = new_top
        mixed = acc[:, :HD] / acc[:, HD:]
        mean_sq = jnp.mean(mixed * mixed, axis=1, keepdims=True)
        normed = mixed * lax.rsqrt(mean_sq + 1e-06) * gain_row[:, h * HD : (h + 1) * HD]
        for i, first in enumerate(firsts):
            obuf[h, pl.ds(first, rows), :] = normed[i * rows : (i + 1) * rows].astype(jnp.bfloat16)

    def send_out(h, step):
        pair, _ = place(step)
        for j in range(2):
            peer = 2 * pair + j
            pltpu.make_async_remote_copy(
                obuf.at[h, pl.ds(pl.multiple_of(peer * tok, tok), tok)],
                out_ref.at[:, pl.ds(pl.multiple_of(me * width + h * HD, HD), HD)],
                out_send, out_recv,
                device_id=(nxt, peer), device_id_type=MESH,
            ).start()

    ahead = lax.rem(me_q, 2) == 1
    behind = jnp.logical_not(ahead)
    last_chip = lax.rem(me_q // 2, RUN) == RUN - 1

    forward_halo(0, 0)
    send_all(keys1)
    forward_halo(0, 1)
    send_all(values1)
    forward_halo(1, 0)

    @pl.when(ahead)
    def _():
        send_all(queries0)

    forward_halo(1, 1)

    @pl.when(behind)
    def _():
        pl.semaphore_wait(go_sem, 1)
        send_all(queries0)

    at_once = jnp.logical_or(behind, last_chip)

    @pl.when(at_once)
    def _():
        send_all(queries1)

    for h in range(HEADS_DEV):
        wait_keys(h)

        if h == 0:

            @pl.when(jnp.logical_and(ahead, jnp.logical_not(last_chip)))
            def _():
                pl.semaphore_signal(go_sem, inc=1, device_id=(prv, me), device_id_type=MESH)

        @pl.loop(0, ny // 2)
        def _(step):
            attend(h, step)
            send_out(h, 2 * step)
            send_out(h, 2 * step + 1)

            if h + 1 < HEADS_DEV:
                @pl.when(jnp.logical_not(at_once))
                def _():
                    @pl.when(step == 0)
                    def _():
                        send_first(*queries1)

                    @pl.when(step > 0)
                    def _():
                        send_pair(*queries1, 2 * step)

                    send_pair(*queries1, 2 * step + 1)

            if h == 0:

                @pl.when(jnp.logical_and(jnp.logical_and(ahead, last_chip), step == 2))
                def _():
                    pl.semaphore_signal(go_sem, inc=1, device_id=(prv, me), device_id_type=MESH)

    for ref, sem in ((q_ref, q_send), (k_ref, k_send), (v_ref, v_send)):
        sent = ref.at[:, pl.ds(0, (ns - 1) * width)]
        pltpu.make_async_copy(sent, sent, sem).wait()
    for h in range(HEADS_DEV):
        for i, buf in enumerate((kbuf, vbuf)):
            halo_copy(buf, h, i).wait_send()
    pltpu.make_async_copy(out_ref, out_ref, out_send).wait()
    pltpu.make_async_copy(out_ref, out_ref, out_recv).wait()


def per_device(query_rows, key_rows, value_rows, level_gains, noise_levels, halo_frames):
    nq, ns = lax.axis_size("queue"), lax.axis_size("seq")
    _, tok, features = query_rows.shape
    group = ns * tok
    flops = 4 * HEADS_DEV * group * (group + EDGE) * HD
    dma = pltpu.SemaphoreType.DMA
    out = pl.pallas_call(
        functools.partial(kernel, nq, ns),
        out_shape=pltpu.VMEM((tok, features), jnp.bfloat16),
        in_specs=[pl.BlockSpec(memory_space=pl.ANY)] * 4
        + [pl.BlockSpec(memory_space=pltpu.SMEM)] * 2,
        out_specs=pl.BlockSpec(memory_space=pl.ANY),
        scratch_shapes=[
            pltpu.VMEM((HEADS_DEV, group, HD), jnp.bfloat16),
            pltpu.VMEM((HEADS_DEV, EDGE + group, HD), jnp.bfloat16),
            pltpu.VMEM((HEADS_DEV, EDGE + group, HD), jnp.bfloat16),
            pltpu.VMEM((HEADS_DEV, group, HD), jnp.bfloat16),
            pltpu.VMEM((LEVELS, HEADS_DEV * HD), jnp.float32),
            dma, dma, dma,
            dma((HEADS_DEV, ns)),
            dma((HEADS_DEV, 2)),
            dma((HEADS_DEV, 2)),
            dma((2, HEADS_DEV)),
            dma((2, HEADS_DEV)),
            dma, dma, dma,
            pltpu.SemaphoreType.REGULAR,
            pltpu.SemaphoreType.REGULAR,
            pltpu.SemaphoreType.REGULAR,
        ],
        compiler_params=pltpu.CompilerParams(
            collective_id=0, has_side_effects=True, vmem_limit_bytes=56 * 2**20
        ),
        cost_estimate=pl.CostEstimate(
            flops=flops, bytes_accessed=8 * 2**20, transcendentals=HEADS_DEV * group * (group + EDGE)
        ),
    )(
        query_rows.reshape(tok, features),
        key_rows.reshape(tok, features),
        value_rows.reshape(tok, features),
        level_gains,
        noise_levels,
        halo_frames,
    )
    return out.reshape(1, tok, features)


def solution(mesh):
    placed = (
        P("queue", "seq", None),
        P("queue", "seq", None),
        P("queue", "seq", None),
        P(),
        P("queue"),
        P("queue"),
    )
    return jax.shard_map(
        per_device, mesh=mesh, in_specs=placed, out_specs=P("queue", "seq", None), check_vma=False
    )
```

```python
import functools
import math

import jax
import jax.numpy as jnp
from jax import lax
from jax.experimental import pallas as pl
from jax.experimental.pallas import tpu as pltpu
from jax.sharding import PartitionSpec as P

HEADS_DEV = 2
HD = 128
FTOK = 128
HALO = 4
LEVELS = 50
EDGE = HALO * FTOK
STAR = 0
RUN = 4
TURNS = (0, 2, 6, 4, 3, 5, 1, 7)
KEY_BLOCK = 1024
MESH = pl.DeviceIdType.MESH
EXP2_SCALE = HD**-0.5 * math.log2(math.e)


def kernel(
    nq,
    ns,
    q_ref,
    k_ref,
    v_ref,
    gains_ref,
    level_ref,
    halo_ref,
    out_ref,
    qbuf,
    kbuf,
    vbuf,
    obuf,
    gbuf,
    q_send,
    k_send,
    v_send,
    q_recv,
    k_recv,
    v_recv,
    halo_send,
    halo_recv,
    out_send,
    out_recv,
    gain_sem,
    ready_sem,
    star_sem,
    go_sem,
):
    tok = q_ref.shape[0]
    width = HEADS_DEV * HD
    tail = EDGE // tok
    me_q = lax.axis_index("queue")
    me = lax.axis_index("seq")
    nxt = lax.rem(me_q + 1, nq)
    prv = lax.rem(me_q + nq - 1, nq)

    barrier = pltpu.get_barrier_semaphore()
    is_star = me == STAR

    @pl.loop(1, ns)
    def _(step):
        peer = lax.rem(me + step, ns)

        @pl.when(peer != STAR)
        def _():
            pl.semaphore_signal(barrier, inc=1, device_id=(me_q, peer), device_id_type=MESH)

    gain_copy = pltpu.make_async_copy(
        gains_ref.at[:, pl.ds(pl.multiple_of(me * width, width), width)], gbuf, gain_sem
    )
    gain_copy.start()

    @pl.when(is_star)
    def _():
        pl.semaphore_signal(barrier, inc=1, device_id=(nxt, STAR), device_id_type=MESH)
        pl.semaphore_wait(star_sem, ns - 1)

    @pl.when(jnp.logical_not(is_star))
    def _():
        pl.semaphore_wait(barrier, ns - 1)
        pl.semaphore_signal(star_sem, inc=1, device_id=(me_q, STAR), device_id_type=MESH)

    is_tail = (me >= ns - tail).astype(jnp.int32)
    ny = ns // 2
    row, side = me // 2, lax.rem(me, 2)

    def offset(step):
        return sum(jnp.where(step == i, turn, 0) for i, turn in enumerate(TURNS))

    def kv_dst(buf, h, source):
        return buf.at[h, pl.ds(pl.multiple_of(EDGE + source * tok, tok), tok)]

    def q_dst(buf, h, source):
        return buf.at[h, pl.ds(pl.multiple_of(source * tok, tok), tok)]

    def src(ref, h, target):
        return ref.at[:, pl.ds(pl.multiple_of(target * width + h * HD, HD), HD)]

    def send(ref, buf, dst, sem, done, h, peer):
        pltpu.make_async_remote_copy(
            src(ref, h, peer), dst(buf, h, me), sem, done, device_id=(me_q, peer), device_id_type=MESH
        ).start()

    def send_pair(ref, buf, dst, sem, done, h, step):
        pair = lax.rem(row + offset(step), ny)
        send(ref, buf, dst, sem, done, h, 2 * pair + side)
        send(ref, buf, dst, sem, done, h, 2 * pair + 1 - side)

    def send_first(ref, buf, dst, sem, done, h):
        pltpu.make_async_copy(src(ref, h, me), dst(buf, h, me), done).start()
        send(ref, buf, dst, sem, done, h, 2 * row + 1 - side)

    def parts(h):
        return (
            (k_ref, kbuf, kv_dst, k_send, k_recv.at[h, is_tail], h),
            (v_ref, vbuf, kv_dst, v_send, v_recv.at[h, is_tail], h),
            (q_ref, qbuf, q_dst, q_send, q_recv.at[h, me], h),
        )

    def send_all(part):
        send_first(*part)

        @pl.loop(1, ny)
        def _(step):
            send_pair(*part, step)

    (keys0, values0, queries0), (keys1, values1, queries1) = parts(0), parts(1)
    send_all(keys0)
    send_all(values0)

    @pl.when(is_star)
    def _():
        pl.semaphore_wait(barrier, 1)
        pl.semaphore_signal(ready_sem, inc=1, device_id=(prv, STAR), device_id_type=MESH)
        pl.semaphore_wait(ready_sem, 1)

        @pl.loop(1, ns)
        def _(step):
            pl.semaphore_signal(
                ready_sem, inc=1, device_id=(me_q, lax.rem(me + step, ns)), device_id_type=MESH
            )

    @pl.when(jnp.logical_not(is_star))
    def _():
        pl.semaphore_wait(ready_sem, 1)

    gain_copy.wait()
    gain_row = gbuf[pl.ds(level_ref[0], 1), :]
    first_seen = jnp.where(me_q > 0, HALO - halo_ref[0], HALO)
    frames = lax.broadcasted_iota(jnp.int32, (1, EDGE), 1) // FTOK
    bias = jnp.where(frames >= first_seen, jnp.float32(0), jnp.float32(-1e30))

    def wait_rows(sem, buf, h, first, rows):
        part = buf.at[h, pl.ds(first, rows)]
        pltpu.make_async_copy(part, part, sem).wait()

    def halo_copy(buf, h, i):
        return pltpu.make_async_remote_copy(
            buf.at[h, pl.ds(ns * tok, EDGE)], buf.at[h, pl.ds(0, EDGE)],
            halo_send.at[i, h], halo_recv.at[i, h],
            device_id=(nxt, me), device_id_type=MESH,
        )

    rows = 2 * tok
    keys_all = EDGE + ns * tok

    def place(step):
        pair = lax.rem(row + 2 * ny - offset(step), ny)
        return pair, pl.multiple_of(pair * rows, rows)

    def forward_halo(h, i):
        buf, recv = ((kbuf, k_recv), (vbuf, v_recv))[i]
        wait_rows(recv.at[h, 1], buf, h, ns * tok, EDGE)
        halo_copy(buf, h, i).start()

    def wait_keys(h):
        for i, (buf, recv) in enumerate(((kbuf, k_recv), (vbuf, v_recv))):
            wait_rows(recv.at[h, 0], buf, h, EDGE, ns * tok - EDGE)
            halo_copy(buf, h, i).wait_recv()

    def attend(h, step):
        firsts = []
        for i in range(2):
            pair, first = place(2 * step + i)
            firsts.append(first)
            for j in range(2):
                part = q_dst(qbuf, h, 2 * pair + j)
                pltpu.make_async_copy(part, part, q_recv.at[h, 2 * pair + j]).wait()
        queries = jnp.concatenate([qbuf[h, pl.ds(first, rows), :] for first in firsts], axis=0)
        acc = top = None
        for start in range(0, keys_all, KEY_BLOCK):
            size = min(KEY_BLOCK, keys_all - start)
            scores = lax.dot_general(
                queries, kbuf[h, start : start + size], (((1,), (1,)), ((), ())),
                preferred_element_type=jnp.float32,
            )
            if start == 0:
                scores = jnp.concatenate([scores[:, :EDGE] + bias, scores[:, EDGE:]], axis=1)
            peak = jnp.max(scores, axis=1, keepdims=True)
            new_top = peak if top is None else jnp.maximum(top, peak)
            weights = jnp.exp2((scores - new_top) * EXP2_SCALE).astype(jnp.bfloat16)
            values = jnp.concatenate(
                [vbuf[h, start : start + size], jnp.ones((size, HD), jnp.bfloat16)], axis=1
            )
            part = jnp.dot(weights, values, preferred_element_type=jnp.float32)
            acc = part if acc is None else acc * jnp.exp2((top - new_top) * EXP2_SCALE) + part
            top = new_top
        mixed = acc[:, :HD] / acc[:, HD:]
        mean_sq = jnp.mean(mixed * mixed, axis=1, keepdims=True)
        normed = mixed * lax.rsqrt(mean_sq + 1e-06) * gain_row[:, h * HD : (h + 1) * HD]
        for i, first in enumerate(firsts):
            obuf[h, pl.ds(first, rows), :] = normed[i * rows : (i + 1) * rows].astype(jnp.bfloat16)

    def send_out(h, step):
        pair, _ = place(step)
        for j in range(2):
            peer = 2 * pair + j
            pltpu.make_async_remote_copy(
                obuf.at[h, pl.ds(pl.multiple_of(peer * tok, tok), tok)],
                out_ref.at[:, pl.ds(pl.multiple_of(me * width + h * HD, HD), HD)],
                out_send, out_recv,
                device_id=(nxt, peer), device_id_type=MESH,
            ).start()

    ahead = lax.rem(me_q, 2) == 1
    behind = jnp.logical_not(ahead)
    last_chip = lax.rem(me_q // 2, RUN) == RUN - 1

    forward_halo(0, 0)
    send_all(keys1)
    forward_halo(0, 1)
    send_all(values1)
    forward_halo(1, 0)

    @pl.when(ahead)
    def _():
        send_all(queries0)

    forward_halo(1, 1)

    @pl.when(behind)
    def _():
        pl.semaphore_wait(go_sem, 1)
        send_all(queries0)

    send_all(queries1)

    for h in range(HEADS_DEV):
        wait_keys(h)

        if h == 0:

            @pl.when(jnp.logical_and(ahead, jnp.logical_not(last_chip)))
            def _():
                pl.semaphore_signal(go_sem, inc=1, device_id=(prv, me), device_id_type=MESH)

        @pl.loop(0, ny // 2)
        def _(step):
            attend(h, step)
            send_out(h, 2 * step)
            send_out(h, 2 * step + 1)

            if h == 0:

                @pl.when(jnp.logical_and(jnp.logical_and(ahead, last_chip), step == 2))
                def _():
                    pl.semaphore_signal(go_sem, inc=1, device_id=(prv, me), device_id_type=MESH)

    for ref, sem in ((q_ref, q_send), (k_ref, k_send), (v_ref, v_send)):
        sent = ref.at[:, pl.ds(0, (ns - 1) * width)]
        pltpu.make_async_copy(sent, sent, sem).wait()
    for h in range(HEADS_DEV):
        for i, buf in enumerate((kbuf, vbuf)):
            halo_copy(buf, h, i).wait_send()
    pltpu.make_async_copy(out_ref, out_ref, out_send).wait()
    pltpu.make_async_copy(out_ref, out_ref, out_recv).wait()


def per_device(query_rows, key_rows, value_rows, level_gains, noise_levels, halo_frames):
    nq, ns = lax.axis_size("queue"), lax.axis_size("seq")
    _, tok, features = query_rows.shape
    group = ns * tok
    flops = 4 * HEADS_DEV * group * (group + EDGE) * HD
    dma = pltpu.SemaphoreType.DMA
    out = pl.pallas_call(
        functools.partial(kernel, nq, ns),
        out_shape=pltpu.VMEM((tok, features), jnp.bfloat16),
        in_specs=[pl.BlockSpec(memory_space=pl.ANY)] * 4
        + [pl.BlockSpec(memory_space=pltpu.SMEM)] * 2,
        out_specs=pl.BlockSpec(memory_space=pl.ANY),
        scratch_shapes=[
            pltpu.VMEM((HEADS_DEV, group, HD), jnp.bfloat16),
            pltpu.VMEM((HEADS_DEV, EDGE + group, HD), jnp.bfloat16),
            pltpu.VMEM((HEADS_DEV, EDGE + group, HD), jnp.bfloat16),
            pltpu.VMEM((HEADS_DEV, group, HD), jnp.bfloat16),
            pltpu.VMEM((LEVELS, HEADS_DEV * HD), jnp.float32),
            dma, dma, dma,
            dma((HEADS_DEV, ns)),
            dma((HEADS_DEV, 2)),
            dma((HEADS_DEV, 2)),
            dma((2, HEADS_DEV)),
            dma((2, HEADS_DEV)),
            dma, dma, dma,
            pltpu.SemaphoreType.REGULAR,
            pltpu.SemaphoreType.REGULAR,
            pltpu.SemaphoreType.REGULAR,
        ],
        compiler_params=pltpu.CompilerParams(
            collective_id=0, has_side_effects=True, vmem_limit_bytes=56 * 2**20
        ),
        cost_estimate=pl.CostEstimate(
            flops=flops, bytes_accessed=8 * 2**20, transcendentals=HEADS_DEV * group * (group + EDGE)
        ),
    )(
        query_rows.reshape(tok, features),
        key_rows.reshape(tok, features),
        value_rows.reshape(tok, features),
        level_gains,
        noise_levels,
        halo_frames,
    )
    return out.reshape(1, tok, features)


def solution(mesh):
    placed = (
        P("queue", "seq", None),
        P("queue", "seq", None),
        P("queue", "seq", None),
        P(),
        P("queue"),
        P("queue"),
    )
    return jax.shard_map(
        per_device, mesh=mesh, in_specs=placed, out_specs=P("queue", "seq", None), check_vma=False
    )
```
